1024 devices in a mesh: row: 16 (over x, z_hi, core), col: 64 (over z_lo, y).
Axes of the slice: x: 4, y: 4, z: 32 (z_hi: 2, z_lo: 16; z = z_hi * 16 + z_lo), core: 2. Of those that a mesh axis runs over, the one named last changes fastest.
Arguments:
- integrals: bfloat16 [2048, 768, 768], P(('row', 'col')), may hold values from -0.875 to 0.875
- block_mask: int32 [2048, 6, 6], P(('row', 'col')), may hold values 0 or 1
- block_sizes: int32 [6], replicated, may hold values from 64 to 128
- density: bfloat16 [768, 768], P('col'), may hold values from -0.21875 to 0.21875
Outputs:
- exchange: float32 [768, 768], P('row', 'col')
The draws below stay inside these ranges and needn't reach their ends.
All inputs are finite; a program needn't handle non-finite values. No bound on the sum of `block_mask` on one device may be relied on, other than what follows from the above.
Results may differ from the reference program's by a relative error of at most 0.0029.
Values may be sent and summed in bfloat16 or wider, within the bound.
A program may use at most 32 MiB of HBM per device.

```python
import jax
import jax.numpy as jnp
from jax import lax

BW = 128
NBLK = 6
NB = 768
NP = 2048


def place_ends(array, stream_key, low, largest):
    shape = array.shape
    index_at = [jax.random.randint(jax.random.fold_in(stream_key, axis), (), 0, shape[axis]) for axis in range(len(shape))]
    array = array.at[tuple(index_at)].set(low)
    longest = shape.index(max(shape))
    index_at[longest] = (index_at[longest] + 1) % shape[longest]
    return array.at[tuple(index_at)].set(largest)


def raised(drawn, rng, source, target, blocks, factor):
    def block_of(position):
        return (jnp.arange(drawn.shape[position]) // (drawn.shape[position] // blocks)).reshape((-1,) + (1,) * (drawn.ndim - 1 - position))

    near = jax.random.permutation(rng, blocks)[block_of(target)]
    other_side = (block_of(target) + blocks // 2) % blocks
    return jnp.where((block_of(source) == near) | (block_of(source) == other_side), factor * drawn, drawn)


def levels(rng, extent, pieces, least, largest):
    def one(position, parts):
        heights = jax.random.uniform(jax.random.fold_in(jax.random.fold_in(rng, 6), position), (parts,), jnp.float32, least / len(pieces), largest / len(pieces))
        return jnp.repeat(jnp.exp(heights), extent[position] // parts).reshape((-1,) + (1,) * (len(extent) - position - 1))

    gain = one(*pieces[0])
    for cut in pieces[1:]:
        gain = gain * one(*cut)
    return gain


def scatter_about(key, shape, scale, most, pieces=(), kind=jnp.bfloat16):
    values = jax.random.normal(key, shape, jnp.float32) * scale
    if len(pieces) > 0:
        values = levels(key, shape, pieces, -0.22, 0.18) * values
    return jnp.clip(values, min=-most, max=most).astype(kind)


def heavy_noise(key, dims, width, reach, split, heavy, held_as=jnp.bfloat16):
    values = width * jax.random.normal(key, dims, jnp.float32)
    if split:
        values = values * levels(key, dims, split, -0.22, 0.18)
    return jnp.clip(raised(values, jax.random.fold_in(key, 3), *heavy), -reach, reach).astype(held_as)


def setup_inputs(seed: int = 0) -> dict:
    arg_keys = jax.random.split(jax.random.key(seed), 5)
    return {
        "integrals": heavy_noise(arg_keys[0], (NP, NB, NB), NB ** -0.5, 0.875, ((0, 1024),), (0, 1, 256, 6.0)),
        "block_mask": place_ends((jax.random.randint(arg_keys[1], (NP, NBLK, NBLK), 0, 4) < 3).astype(jnp.int32), jax.random.fold_in(arg_keys[1], 1), 0, 1),
        "block_sizes": place_ends(jax.random.randint(arg_keys[2], (NBLK,), BW // 2, BW + 1), jax.random.fold_in(arg_keys[2], 1), BW // 2, BW).astype(jnp.int32),
        "density": scatter_about(arg_keys[3], (NB, NB), NB ** -0.5, 0.21875, ((0, 64),)),
    }


def present_columns(block_sizes):
    index = jnp.arange(NB, dtype=jnp.int32)
    owners = jnp.repeat(block_sizes, BW)
    return (index % BW < owners).astype(jnp.int32)


def reference(integrals, block_mask, block_sizes, density):
    present = present_columns(block_sizes)
    outer = present[:, None] * present[None, :]

    def accumulate(carried, items):
        slab, screen = items
        expanded = jnp.repeat(jnp.repeat(screen, BW, 0), BW, 1) * outer
        screened = slab * expanded.astype(slab.dtype)
        contracted = jnp.dot(screened, density, preferred_element_type=jnp.float32).astype(jnp.bfloat16)
        return carried + jnp.dot(contracted, screened.T, preferred_element_type=jnp.float32), None

    start_value = jnp.zeros((NB, NB), jnp.float32)
    exchange, unused = lax.scan(accumulate, start_value, (integrals, block_mask))
    return exchange
```

```python
import jax
import jax.numpy as jnp
from jax import lax
from jax.experimental import pallas as pl
from jax.experimental.pallas import tpu as pltpu
from jax.sharding import PartitionSpec as P

MESH = pl.DeviceIdType.MESH
F32 = jnp.float32
BF16 = jnp.bfloat16

Z_GATHER = [d for d in range(-8, 8) if d != 0]
PLANE = [(dx, dy) for dx in range(4) for dy in range(4) if (dx, dy) != (0, 0)]
Z_NEAR = [-2, -1, 1]
Z_FAR = [-12, -8, -4, 4, 8, 12, 16]
Z_GREET = [d for d in range(-8, 9) if d != 0] + [-12, 12, 16]


def device(x, y, z, core):
    return ((x * 2 + z // 16) * 2 + core, (z % 16) * 4 + y)


def wrap(value, size):
    return lax.rem(value + size, size)


def iota(shape, dim):
    return lax.broadcasted_iota(jnp.int32, shape, dim)


def dot(a, b):
    return jnp.dot(a, b, preferred_element_type=F32)


def dot_nt(a, b):
    return lax.dot_general(a, b, (((1,), (1,)), ((), ())), preferred_element_type=F32)


def kernel(
    mask_ref, sizes_ref, integrals_ref, density_ref, out_ref,
    raw, screened, left, right, swap, spread, squeeze, tile, dens, contracted,
    k_send, k_land, p_send, p_land, by_column, n_land, f_send, f_land,
    load_sem, zs, zr, ps, pr, cs, cr, ks, kr, qs, qr, ns, nr, fs, fr,
):
    row, col = lax.axis_index("row"), lax.axis_index("col")
    x, y = row // 4, col % 4
    z, core = (row // 2) % 2 * 16 + col // 4, row % 2
    z_lo = col // 4
    sibling = device(x, y, z, 1 - core)

    def at_z(d):
        return device(x, y, wrap(z + d, 32), core)

    def in_plane(dx, dy):
        return device((x + dx) % 4, (y + dy) % 4, z, core)

    def remote(src, dst, send, recv, target):
        return pltpu.make_async_remote_copy(
            src_ref=src, dst_ref=dst, send_sem=send, recv_sem=recv,
            device_id=target, device_id_type=MESH,
        )

    barrier = pltpu.get_barrier_semaphore()
    greet = [at_z(d) for d in Z_GREET] + [in_plane(*d) for d in PLANE] + [sibling]
    for target in greet:
        pl.semaphore_signal(barrier, inc=1, device_id=target, device_id_type=MESH)

    load = pltpu.make_async_copy(integrals_ref, raw, load_sem)
    load.start()

    slot = z_lo % 4 * 4 + z_lo // 4
    column = pl.multiple_of(core * 384 + lax.rem(x, 3) * 128, 128)
    pad = (iota((16, 12), 0) == iota((16, 12), 1)).astype(BF16)
    tile[slot] = dot(pad, density_ref[:, pl.ds(column, 128)]).astype(BF16)

    r, c = iota((192, 256), 0), iota((192, 256), 1)
    squeeze[...] = ((r // 12) * 16 + r % 12 == c).astype(BF16)

    @pl.loop(0, 6)
    def _(i):
        start = pl.multiple_of(i * 128, 128)
        r, c = iota((128, 768), 0) + start, iota((128, 768), 1)
        moved = r % 192 // 12 % 4 * 192 + r % 192 // 48 * 48 + r // 192 * 12 + r % 12
        swap[pl.ds(start, 128)] = (moved == c).astype(BF16)
        tail = r - 512
        part = jnp.where(r < 512, r // 128, tail // 64)
        q = jnp.where(r < 512, r % 128, tail % 64 + 128)
        source = q % 48 // 12 * 192 + q // 48 * 48 + part * 12 + q % 12
        spread[pl.ds(start, 128)] = (source == c).astype(BF16)

    load.wait()

    lane = iota((1, 128), 1)
    for i in range(6):
        present_row = (iota((128, 128), 0) < sizes_ref[i]).astype(F32).astype(BF16)
        for p in range(2):
            for k in range(6):
                keep = (lane < sizes_ref[k] * mask_ref[p, i, k]).astype(F32).astype(BF16)
                block = raw[p, pl.ds(i * 128, 128), pl.ds(k * 128, 128)]
                screened[p, pl.ds(i * 128, 128), pl.ds(k * 128, 128)] = block * (present_row * keep)

    pl.semaphore_wait(barrier, len(greet))

    z_copies = [
        remote(tile.at[slot], tile.at[slot], zs.at[n], zr.at[n], at_z(d))
        for n, d in enumerate(Z_GATHER)
    ]

    @pl.when(x < 3)
    def _():
        for copy in z_copies:
            copy.start()

    @pl.loop(0, 8)
    def _(i):
        p, part = i // 4, i % 4
        rows = pl.ds(pl.multiple_of(part * 192, 192), 192)
        moved = dot(screened[p, rows], swap[...]).astype(BF16)
        for zh in range(2):
            for other in range(2):
                half = (other + core + 1) % 2
                to = pl.multiple_of(half * 384 + part * 96 + zh * 48, 16)
                at = zh * 96 + other * 48
                left[p, pl.ds(to, 48)] = moved[at : at + 48]
        right[p, rows] = dot(spread[rows], screened[p]).astype(BF16)

    @pl.when(x < 3)
    def _():
        for copy in z_copies:
            copy.wait()
        mine = pl.ds(pl.multiple_of(y * 192, 16), 192)
        dens[core, x, mine] = dot(squeeze[...], tile[...].reshape(256, 128)).astype(BF16)
        for n, (dx, dy) in enumerate(PLANE):
            remote(
                dens.at[core, x, mine], dens.at[core, x, mine], ps.at[n], pr.at[x * 4 + y],
                in_plane(dx, dy),
            ).start()

    for sx in range(3):
        for sy in range(4):
            n = sx * 4 + sy
            block = dens.at[core, sx, pl.ds(sy * 192, 192)]

            @pl.when(jnp.logical_or(x != sx, y != sy))
            def _():
                remote(block, block, ps.at[0], pr.at[n], sibling).wait_recv()

            remote(block, block, cs.at[n], cr.at[n], sibling).start()

    def contract(half):
        density = jnp.concatenate([dens[half, t] for t in range(3)], axis=1)

        @pl.loop(0, 4)
        def _(i):
            p, rows = i // 2, pl.ds(pl.multiple_of(i % 2 * 384, 384), 384)
            contracted[p, half, rows] = dot(left[p, rows], density).astype(BF16)

    contract(core)
    for sx in range(3):
        for sy in range(4):
            n = sx * 4 + sy
            block = dens.at[1 - core, sx, pl.ds(sy * 192, 192)]
            remote(block, block, cs.at[n], cr.at[n], sibling).wait_recv()
    contract(1 - core)

    def exchange(half, chunk):
        total = None
        for p in range(2):
            rows = pl.ds(half * 384, 384)
            a = jnp.concatenate([contracted[p, 0, rows], contracted[p, 1, rows]], axis=1)
            term = dot_nt(a, right[p, pl.ds(chunk * 256, 256)])
            total = term if total is None else total + term
        return total

    k_copies = [
        remote(k_send.at[n], k_land.at[n], ks.at[n], kr.at[n], sibling) for n in range(3)
    ]
    for n in range(3):
        k_send[n] = exchange(0, n).astype(BF16)
        k_copies[n].start()
    low = iota((48, 128), 1) < 64
    for n in range(3):
        own = exchange(1, n)
        k_copies[n].wait_recv()
        total = own + k_land[n].astype(F32)
        for tx in range(4):
            for half in range(2):
                block = total[tx * 96 : tx * 96 + 96, half * 128 : half * 128 + 128]
                if n < 2:
                    p_send[tx * 4 + n * 2 + half, :96] = block.astype(BF16)
                else:
                    first, second = block[:48], block[48:]
                    even = jnp.where(low, first, pltpu.roll(second, 64, 1))
                    odd = jnp.where(low, pltpu.roll(first, 64, 1), second)
                    p_send[tx * 4 + half * 2, 96:] = even.astype(BF16)
                    p_send[tx * 4 + half * 2 + 1, 96:] = odd.astype(BF16)

    q_copies = []
    for n, (dx, dy) in enumerate(PLANE):
        target = (x + dx) % 4 * 4 + (y + dy) % 4
        q_copies.append(
            remote(p_send.at[target], p_land.at[n], qs.at[n], qr.at[n], in_plane(dx, dy))
        )
        q_copies[-1].start()
    total = p_send[x * 4 + y].astype(F32)
    for n, copy in enumerate(q_copies):
        copy.wait_recv()
        total = total + p_land[n].astype(F32)

    zeros = jnp.zeros((80, 128), F32)
    by_column[:128] = jnp.transpose(jnp.concatenate([total[:96], zeros[:32]], axis=0))
    turned = jnp.transpose(jnp.concatenate([total[96:], zeros], axis=0))
    lanes = iota((64, 128), 1)
    by_column[128:] = jnp.where(lanes < 48, turned[:64], pltpu.roll(turned[64:], 48, 1))

    n_copies = []
    for n, d in enumerate(Z_NEAR):
        at = pl.multiple_of((z + d + 32) % 4 * 48, 16)
        n_copies.append(
            remote(by_column.at[pl.ds(at, 48)], n_land.at[n], ns.at[n], nr.at[n], at_z(d))
        )
        n_copies[-1].start()
    total = by_column[pl.ds(pl.multiple_of(z % 4 * 48, 16), 48)]
    for n, copy in enumerate(n_copies):
        copy.wait_recv()
        total = total + n_land[n]

    lanes = iota((8, 128), 1)
    for b in range(4):
        first = total[b * 12 : b * 12 + 8]
        second = jnp.concatenate([total[b * 12 + 8 : b * 12 + 12]] * 2, axis=0)
        f_send[b] = jnp.where(lanes < 48, first, pltpu.roll(second, 48, 1))
        f_send[4 + b] = jnp.where(lanes < 48, pltpu.roll(first, 80, 1), second)
    f_copies = []
    for n, d in enumerate(Z_FAR):
        target = wrap(z + d, 32) // 4
        f_copies.append(
            remote(f_send.at[target], f_land.at[n], fs.at[n], fr.at[n], at_z(d))
        )
        f_copies[-1].start()
    total = f_send[z // 4]
    for n, copy in enumerate(f_copies):
        copy.wait_recv()
        total = total + f_land[n]
    turned = jnp.transpose(jnp.concatenate([total, jnp.zeros((120, 128), F32)], axis=0))
    out_ref[:, :8] = turned[:48, :8]
    out_ref[:, 8:] = turned[48:96, :4]

    @pl.when(x < 3)
    def _():
        mine = pl.ds(pl.multiple_of(y * 192, 16), 192)
        for n, (dx, dy) in enumerate(PLANE):
            remote(
                dens.at[core, x, mine], dens.at[core, x, mine], ps.at[n], pr.at[x * 4 + y],
                in_plane(dx, dy),
            ).wait_send()

    for n in range(12):
        block = dens.at[core, n // 4, pl.ds(n % 4 * 192, 192)]
        remote(block, block, cs.at[n], cr.at[n], sibling).wait_send()
    for copy in k_copies + q_copies + n_copies + f_copies:
        copy.wait_send()


def shards(integrals, block_mask, block_sizes, density):
    dma = lambda n: pltpu.SemaphoreType.DMA((n,))
    vmem = lambda *shape: pltpu.VMEM(shape, BF16)
    return pl.pallas_call(
        kernel,
        out_shape=jax.ShapeDtypeStruct((48, 12), F32),
        in_specs=[
            pl.BlockSpec(memory_space=pltpu.SMEM),
            pl.BlockSpec(memory_space=pltpu.SMEM),
            pl.BlockSpec(memory_space=pl.ANY),
            pl.BlockSpec(memory_space=pltpu.VMEM),
        ],
        out_specs=pl.BlockSpec(memory_space=pltpu.VMEM),
        scratch_shapes=[
            vmem(2, 768, 768),
            vmem(2, 768, 768),
            vmem(2, 768, 768),
            vmem(2, 768, 768),
            vmem(768, 768),
            vmem(768, 768),
            vmem(192, 256),
            vmem(16, 16, 128),
            vmem(2, 3, 768, 128),
            vmem(2, 2, 768, 384),
            vmem(3, 384, 256),
            vmem(3, 384, 256),
            vmem(16, 144, 128),
            vmem(15, 144, 128),
            pltpu.VMEM((192, 128), F32),
            pltpu.VMEM((3, 48, 128), F32),
            pltpu.VMEM((8, 8, 128), F32),
            pltpu.VMEM((7, 8, 128), F32),
            pltpu.SemaphoreType.DMA,
            dma(15), dma(15),
            dma(15), dma(12),
            dma(12), dma(12),
            dma(3), dma(3),
            dma(15), dma(15),
            dma(3), dma(3),
            dma(7), dma(7),
        ],
        compiler_params=pltpu.CompilerParams(
            collective_id=0, has_side_effects=True, vmem_limit_bytes=48 * 1024 * 1024
        ),
        name="exchange",
    )(block_mask, block_sizes, integrals, density)


def solution(mesh):
    return jax.shard_map(
        shards,
        mesh=mesh,
        in_specs=(
            P(("row", "col"), None, None),
            P(("row", "col"), None, None),
            P(),
            P("col", None),
        ),
        out_specs=P("row", "col"),
        check_vma=False,
    )
```

```python
import jax
import jax.numpy as jnp
from jax import lax
from jax.experimental import pallas as pl
from jax.experimental.pallas import tpu as pltpu
from jax.sharding import PartitionSpec as P

MESH = pl.DeviceIdType.MESH
F32 = jnp.float32
BF16 = jnp.bfloat16

Z_SLOTS = [n - 4 if n < 12 else n - 20 for n in range(16)]
Z_OWN = Z_SLOTS.index(0)
PLANE = [(dx, dy) for dx in range(4) for dy in range(4) if (dx, dy) != (0, 0)]
Z_NEAR = [-2, -1, 1]
Z_FAR = [-12, -8, -4, 4, 8, 12, 16]
Z_GREET = sorted((d for d in range(-8, 9) if d != 0), key=lambda d: -abs(d))


def device(x, y, z, core):
    return ((x * 2 + z // 16) * 2 + core, (z % 16) * 4 + y)


def wrap(value, size):
    return lax.rem(value + size, size)


def iota(shape, dim):
    return lax.broadcasted_iota(jnp.int32, shape, dim)


def dot(a, b):
    return jnp.dot(a, b, preferred_element_type=F32)


def dot_nt(a, b):
    return lax.dot_general(a, b, (((1,), (1,)), ((), ())), preferred_element_type=F32)


def kernel(
    mask_hbm, sizes_hbm, integrals_ref, density_hbm, out_ref,
    mask_ref, sizes_ref, density_ref,
    raw, screened, left, right, swap, spread, squeeze, tile, own3, tile3, dens, contracted,
    k_send, k_land, p_send, p_land, by_column, n_land, f_send, f_land,
    load_sem, ready, zs, zr, ps, pr, cs, cr, ks, kr, qs, qr, ns, nr, fs, fr,
):
    row, col = lax.axis_index("row"), lax.axis_index("col")
    x, y = row // 4, col % 4
    z, core = (row // 2) % 2 * 16 + col // 4, row % 2
    z_lo = col // 4
    sibling = device(x, y, z, 1 - core)

    def at_z(d):
        return device(x, y, wrap(z + d, 32), core)

    def in_plane(dx, dy):
        return device((x + dx) % 4, (y + dy) % 4, z, core)

    def remote(src, dst, send, recv, target):
        return pltpu.make_async_remote_copy(
            src_ref=src, dst_ref=dst, send_sem=send, recv_sem=recv,
            device_id=target, device_id_type=MESH,
        )

    barrier = pltpu.get_barrier_semaphore()
    greet = [at_z(d) for d in Z_GREET] + [in_plane(*d) for d in PLANE] + [sibling]
    for target in greet:
        pl.semaphore_signal(barrier, inc=1, device_id=target, device_id_type=MESH)

    loads = [
        pltpu.make_async_copy(density_hbm, density_ref, load_sem.at[0]),
        pltpu.make_async_copy(sizes_hbm, sizes_ref, load_sem.at[1]),
        pltpu.make_async_copy(mask_hbm, mask_ref, load_sem.at[2]),
        pltpu.make_async_copy(integrals_ref, raw, load_sem.at[3]),
    ]
    for load in loads:
        load.start()

    r, c = iota((96, 128), 0), iota((96, 128), 1)
    squeeze[...] = ((r // 12) * 16 + r % 12 == c).astype(BF16)

    loads[0].wait()
    pad = (iota((16, 12), 0) == iota((16, 12), 1)).astype(BF16)
    for t in range(3):
        column = pl.multiple_of(core * 384 + t * 128, 128)
        own3[t] = dot(pad, density_ref[:, pl.ds(column, 128)]).astype(BF16)
    tile[Z_OWN] = own3[lax.rem(x, 3)]

    for load in loads[1:]:
        load.wait()

    lane = iota((1, 128), 1)
    for i in range(6):
        present_row = (iota((128, 128), 0) < sizes_ref[i]).astype(F32).astype(BF16)
        for p in range(2):
            for k in range(6):
                keep = (lane < sizes_ref[k] * mask_ref[i, p, k]).astype(F32).astype(BF16)
                block = raw[p, pl.ds(i * 128, 128), pl.ds(k * 128, 128)]
                screened[p, pl.ds(i * 128, 128), pl.ds(k * 128, 128)] = block * (present_row * keep)

    pl.semaphore_wait(barrier, len(greet))
    for d in (-8, 8):
        pl.semaphore_signal(ready, inc=1, device_id=at_z(d), device_id_type=MESH)

    def z_copy(n):
        if n < 12:
            return remote(tile.at[Z_OWN], tile.at[n], zs.at[n], zr.at[n], at_z(Z_SLOTS[n]))
        return remote(own3, tile3.at[n - 12], zs.at[n], zr.at[n], at_z(Z_SLOTS[n]))

    @pl.when(x < 3)
    def _():
        for n in sorted(range(12), key=lambda n: -abs(Z_SLOTS[n])):
            if n != Z_OWN:
                z_copy(n).start()

    @pl.when(x == 3)
    def _():
        for n in range(12, 16):
            z_copy(n).start()

    @pl.loop(0, 6)
    def _(i):
        start = pl.multiple_of(i * 128, 128)
        r, c = iota((128, 768), 0) + start, iota((128, 768), 1)
        origin = (z_lo + 36 - c // 384 * 8 - c % 96 // 12) % 16
        swap[pl.ds(start, 128)] = (origin * 48 + c % 384 // 96 * 12 + c % 12 == r).astype(BF16)
        tail = r - 512
        part = jnp.where(r < 512, r // 128, tail // 64)
        q = jnp.where(r < 512, r % 128, tail % 64 + 128)
        source = q % 48 // 12 * 192 + q // 48 * 48 + part * 12 + q % 12
        spread[pl.ds(start, 128)] = (source == c).astype(BF16)

    def prepare(p):
        @pl.loop(0, 4)
        def _(part):
            rows = pl.ds(pl.multiple_of(part * 192, 192), 192)
            moved = dot(screened[p, rows], swap[...]).astype(BF16)
            for zh in range(2):
                for other in range(2):
                    half = (other + core + 1) % 2
                    to = pl.multiple_of(half * 384 + part * 96 + zh * 48, 16)
                    at = zh * 96 + other * 48
                    left[p, pl.ds(to, 48)] = moved[at : at + 48]
            right[p, rows] = dot(spread[rows], screened[p]).astype(BF16)

    prepare(0)

    def block(g, sx, sy):
        at = pl.multiple_of(g * 384 + sy * 96, 16)
        return dens.at[core, sx, pl.ds(at, 96 if g == 0 else 48)]

    def block3(sy):
        return dens.at[core, :, pl.ds(pl.multiple_of(384 + sy * 96 + 48, 16), 48)]

    def plane_copy(g, n):
        mine = block(g, x, y)
        return remote(mine, mine, ps.at[g, n], pr.at[g * 12 + x * 4 + y], in_plane(*PLANE[n]))

    def plane_copy3(n):
        mine = block3(y)
        return remote(mine, mine, ps.at[1, n], pr.at[24 + y], in_plane(*PLANE[n]))

    @pl.when(x < 3)
    def _():
        for g in range(2):
            slots = range(8) if g == 0 else range(8, 12)
            for n in slots:
                if n != Z_OWN:
                    z_copy(n).wait()
            size = len(slots)
            rows = tile[slots[0] : slots[0] + size].reshape(size * 16, 128)
            packed = dot(squeeze[: size * 12, : size * 16], rows).astype(BF16)
            dens[core, x, pl.ds(pl.multiple_of(g * 384 + y * 96, 16), size * 12)] = packed
            for n in range(len(PLANE)):
                plane_copy(g, n).start()

    @pl.when(x == 3)
    def _():
        for n in range(12, 16):
            z_copy(n).wait()
        for t in range(3):
            packed = dot(squeeze[:48, :64], tile3[:, t].reshape(64, 128)).astype(BF16)
            dens[core, t, pl.ds(pl.multiple_of(384 + y * 96 + 48, 16), 48)] = packed
        for n in range(len(PLANE)):
            plane_copy3(n).start()

    prepare(1)

    c_copies = []
    for g in range(2):
        if g == 1:
            for sy in range(4):

                @pl.when(jnp.logical_or(x != 3, y != sy))
                def _():
                    remote(block3(sy), block3(sy), ps.at[0, 0], pr.at[24 + sy], sibling).wait_recv()

        for sx in range(3):
            for sy in range(4):

                @pl.when(jnp.logical_or(x != sx, y != sy))
                def _():
                    arrived = block(g, sx, sy)
                    remote(
                        arrived, arrived, ps.at[0, 0], pr.at[g * 12 + sx * 4 + sy], sibling
                    ).wait_recv()

            whole = dens.at[core, sx, pl.ds(g * 384, 384)]
            c_copies.append(remote(whole, whole, cs.at[g * 3 + sx], cr.at[g * 3 + sx], sibling))
            c_copies[-1].start()

    def contract(half):
        density = jnp.concatenate([dens[half, t] for t in range(3)], axis=1)

        @pl.loop(0, 4)
        def _(i):
            p, rows = i // 2, pl.ds(pl.multiple_of(i % 2 * 384, 384), 384)
            contracted[p, half, rows] = dot(left[p, rows], density).astype(BF16)

    contract(core)
    for g in range(2):
        for sx in range(3):
            whole = dens.at[1 - core, sx, pl.ds(g * 384, 384)]
            remote(
                whole, whole, cs.at[g * 3 + sx], cr.at[g * 3 + sx], sibling
            ).wait_recv()
    contract(1 - core)

    def exchange(half, chunk):
        total = None
        for p in range(2):
            rows = pl.ds(half * 384, 384)
            a = jnp.concatenate([contracted[p, 0, rows], contracted[p, 1, rows]], axis=1)
            term = dot_nt(a, right[p, pl.ds(chunk * 256, 256)])
            total = term if total is None else total + term
        return total

    k_copies = [
        remote(k_send.at[n], k_land.at[n], ks.at[n], kr.at[n], sibling) for n in range(3)
    ]
    low = iota((48, 128), 1) < 64

    def send_half(n):
        k_send[n] = exchange(0, n).astype(BF16)
        k_copies[n].start()

    def own_half(n):
        own = exchange(1, n)
        k_copies[n].wait_recv()
        total = own + k_land[n].astype(F32)
        for tx in range(4):
            for half in range(2):
                block = total[tx * 96 : tx * 96 + 96, half * 128 : half * 128 + 128]
                if n < 2:
                    p_send[tx * 4 + n * 2 + half, :96] = block.astype(BF16)
                else:
                    first, second = block[:48], block[48:]
                    even = jnp.where(low, first, pltpu.roll(second, 64, 1))
                    odd = jnp.where(low, pltpu.roll(first, 64, 1), second)
                    p_send[tx * 4 + half * 2, 96:] = even.astype(BF16)
                    p_send[tx * 4 + half * 2 + 1, 96:] = odd.astype(BF16)

    parts = [pl.ds(0, 96), pl.ds(96, 48)]

    def send_plane(part, ty):
        for tx in range(4):

            @pl.when(jnp.logical_or(tx != x, ty != y))
            def _():
                slot = (tx - x + 4) % 4 * 4 + (ty - y + 4) % 4
                remote(
                    p_send.at[tx * 4 + ty, parts[part]], p_land.at[slot, parts[part]],
                    qs.at[part, slot], qr.at[part, slot], device(tx, ty, z, core),
                ).start()

    send_half(0)
    send_half(1)
    own_half(0)
    send_plane(0, 0)
    send_plane(0, 1)
    send_half(2)
    own_half(1)
    send_plane(0, 2)
    send_plane(0, 3)
    own_half(2)
    for ty in range(4):
        send_plane(1, ty)

    q_copies = [
        remote(
            p_send.at[0, rows], p_land.at[slot, rows], qs.at[part, slot], qr.at[part, slot], sibling
        )
        for part, rows in enumerate(parts)
        for slot in range(1, 16)
    ]
    sums = []
    for part, rows in enumerate(parts):
        total = p_send[x * 4 + y, rows].astype(F32)
        for slot in range(1, 16):
            q_copies[part * 15 + slot - 1].wait_recv()
            total = total + p_land[slot, rows].astype(F32)
        sums.append(total)

    zeros = jnp.zeros((80, 128), F32)
    by_column[:128] = jnp.transpose(jnp.concatenate([sums[0], zeros[:32]], axis=0))
    turned = jnp.transpose(jnp.concatenate([sums[1], zeros], axis=0))
    lanes = iota((64, 128), 1)
    by_column[128:] = jnp.where(lanes < 48, turned[:64], pltpu.roll(turned[64:], 48, 1))

    n_copies = []
    for n, d in enumerate(Z_NEAR):
        at = pl.multiple_of((z + d + 32) % 4 * 48, 16)
        n_copies.append(
            remote(by_column.at[pl.ds(at, 48)], n_land.at[n], ns.at[n], nr.at[n], at_z(d))
        )
        n_copies[-1].start()
    total = by_column[pl.ds(pl.multiple_of(z % 4 * 48, 16), 48)]
    for n, copy in enumerate(n_copies):
        copy.wait_recv()
        total = total + n_land[n]

    lanes = iota((8, 128), 1)
    for b in range(4):
        first = total[b * 12 : b * 12 + 8]
        second = jnp.concatenate([total[b * 12 + 8 : b * 12 + 12]] * 2, axis=0)
        f_send[b] = jnp.where(lanes < 48, first, pltpu.roll(second, 48, 1))
        f_send[4 + b] = jnp.where(lanes < 48, pltpu.roll(first, 80, 1), second)
    pl.semaphore_wait(ready, 2)
    f_copies = []
    for n, d in enumerate(Z_FAR):
        target = wrap(z + d, 32) // 4
        f_copies.append(
            remote(f_send.at[target], f_land.at[n], fs.at[n], fr.at[n], at_z(d))
        )
        f_copies[-1].start()
    total = f_send[z // 4]
    for n, copy in enumerate(f_copies):
        copy.wait_recv()
        total = total + f_land[n]
    out_ref[:8] = total[:, :48]
    out_ref[8:] = pltpu.roll(total, 80, 1)[:4, :48]

    @pl.when(x < 3)
    def _():
        for g in range(2):
            for n in range(len(PLANE)):
                plane_copy(g, n).wait_send()

    @pl.when(x == 3)
    def _():
        for n in range(len(PLANE)):
            plane_copy3(n).wait_send()

    for copy in c_copies + k_copies + q_copies + n_copies + f_copies:
        copy.wait_send()


def shards(integrals, block_mask, block_sizes, density):
    dma = lambda *shape: pltpu.SemaphoreType.DMA(shape)
    vmem = lambda *shape: pltpu.VMEM(shape, BF16)
    exchange = pl.pallas_call(
        kernel,
        out_shape=pltpu.VMEM((12, 48), F32),
        in_specs=[pl.BlockSpec(memory_space=pltpu.HBM)] * 4,
        out_specs=pl.BlockSpec(memory_space=pltpu.VMEM),
        scratch_shapes=[
            pltpu.SMEM((6, 2, 6), jnp.int32),
            pltpu.SMEM((6,), jnp.int32),
            vmem(12, 768),
            vmem(2, 768, 768),
            vmem(2, 768, 768),
            vmem(2, 768, 768),
            vmem(2, 768, 768),
            vmem(768, 768),
            vmem(768, 768),
            vmem(96, 128),
            vmem(12, 16, 128),
            vmem(3, 16, 128),
            vmem(4, 3, 16, 128),
            vmem(2, 3, 768, 128),
            vmem(2, 2, 768, 384),
            vmem(3, 384, 256),
            vmem(3, 384, 256),
            vmem(16, 144, 128),
            vmem(16, 144, 128),
            pltpu.VMEM((192, 128), F32),
            pltpu.VMEM((3, 48, 128), F32),
            pltpu.VMEM((8, 8, 128), F32),
            pltpu.VMEM((7, 8, 128), F32),
            dma(4),
            pltpu.SemaphoreType.REGULAR,
            dma(16), dma(16),
            dma(2, 15), dma(28),
            dma(6), dma(6),
            dma(3), dma(3),
            dma(2, 16), dma(2, 16),
            dma(3), dma(3),
            dma(7), dma(7),
        ],
        compiler_params=pltpu.CompilerParams(
            collective_id=0, has_side_effects=True, vmem_limit_bytes=60 * 1024 * 1024
        ),
        name="exchange",
    )(jnp.transpose(block_mask, (1, 0, 2)), block_sizes, integrals, density)
    return jnp.transpose(exchange)


def solution(mesh):
    return jax.shard_map(
        shards,
        mesh=mesh,
        in_specs=(
            P(("row", "col"), None, None),
            P(("row", "col"), None, None),
            P(),
            P("col", None),
        ),
        out_specs=P("row", "col"),
        check_vma=False,
    )
```

```python
import jax
import jax.numpy as jnp
from jax import lax
from jax.experimental import pallas as pl
from jax.experimental.pallas import tpu as pltpu
from jax.sharding import PartitionSpec as P

MESH = pl.DeviceIdType.MESH
F32 = jnp.float32
BF16 = jnp.bfloat16

Z_OWN = 4
PLANE = [(dx, dy) for dx in range(4) for dy in range(4) if (dx, dy) != (0, 0)]
Z_NEAR = [-2, -1, 1]
Z_FAR = [-12, -8, -4, 4, 8, 12, 16]
Z_GREET = [-4, 4, -3, 3, -2, 2, -1, 1]


def device(x, y, z, core):
    return ((x * 2 + z // 16) * 2 + core, (z % 16) * 4 + y)


def wrap(value, size):
    return lax.rem(value + size, size)


def iota(shape, dim):
    return lax.broadcasted_iota(jnp.int32, shape, dim)


def dot(a, b):
    return jnp.dot(a, b, preferred_element_type=F32)


def dot_nt(a, b):
    return lax.dot_general(a, b, (((1,), (1,)), ((), ())), preferred_element_type=F32)


def kernel(
    mask_hbm, sizes_hbm, integrals_ref, density_hbm, out_ref,
    mask_ref, sizes_ref, density_ref,
    raw, screened, left, right, swap, spread, squeeze, tile, dens, contracted,
    k_send, k_land, p_send, p_land, by_column, n_land, f_send, f_land,
    load_sem, ready, ready_far, zs, zr, ps, pr, cs, cr, ks, kr, qs, qr, ns, nr, fs, fr,
):
    row, col = lax.axis_index("row"), lax.axis_index("col")
    x, y = row // 4, col % 4
    z, core = (row // 2) % 2 * 16 + col // 4, row % 2
    z_lo = col // 4
    sibling = device(x, y, z, 1 - core)

    def at_z(d):
        return device(x, y, wrap(z + d, 32), core)

    def in_plane(dx, dy):
        return device((x + dx) % 4, (y + dy) % 4, z, core)

    def remote(src, dst, send, recv, target):
        return pltpu.make_async_remote_copy(
            src_ref=src, dst_ref=dst, send_sem=send, recv_sem=recv,
            device_id=target, device_id_type=MESH,
        )

    barrier = pltpu.get_barrier_semaphore()
    greet = [at_z(d) for d in Z_GREET] + [in_plane(*d) for d in PLANE] + [sibling]
    for target in greet:
        pl.semaphore_signal(barrier, inc=1, device_id=target, device_id_type=MESH)

    loads = [
        pltpu.make_async_copy(density_hbm, density_ref, load_sem.at[0]),
        pltpu.make_async_copy(sizes_hbm, sizes_ref, load_sem.at[1]),
        pltpu.make_async_copy(mask_hbm, mask_ref, load_sem.at[2]),
        pltpu.make_async_copy(integrals_ref, raw, load_sem.at[3]),
    ]
    for load in loads:
        load.start()

    r, c = iota((96, 128), 0), iota((96, 128), 1)
    squeeze[...] = ((r // 12) * 16 + r % 12 == c).astype(BF16)

    loads[0].wait()
    column = pl.multiple_of(core * 384 + lax.rem(x, 3) * 128, 128)
    pad = (iota((16, 12), 0) == iota((16, 12), 1)).astype(BF16)
    tile[Z_OWN] = dot(pad, density_ref[:, pl.ds(column, 128)]).astype(BF16)

    pl.semaphore_wait(barrier, len(greet))
    for d in (-4, 4):
        pl.semaphore_signal(ready, inc=1, device_id=at_z(d), device_id_type=MESH)

    def z_copy(n):
        return remote(tile.at[Z_OWN], tile.at[n], zs.at[n], zr.at[n], at_z(n - 4))

    z_up = remote(tile.at[pl.ds(4, 4)], tile.at[pl.ds(8, 4)], zs.at[8], zr.at[8], at_z(4))
    z_down = remote(tile.at[pl.ds(0, 4)], tile.at[pl.ds(12, 4)], zs.at[9], zr.at[9], at_z(-4))

    @pl.when(x < 3)
    def _():
        for n in (0, 1, 7, 2, 6, 3, 5):
            z_copy(n).start()

    for load in loads[1:]:
        load.wait()

    lane = iota((1, 128), 1)
    for i in range(6):
        present_row = (iota((128, 128), 0) < sizes_ref[i]).astype(F32).astype(BF16)
        for p in range(2):
            for k in range(6):
                keep = (lane < sizes_ref[k] * mask_ref[i, p, k]).astype(F32).astype(BF16)
                block = raw[p, pl.ds(i * 128, 128), pl.ds(k * 128, 128)]
                screened[p, pl.ds(i * 128, 128), pl.ds(k * 128, 128)] = block * (present_row * keep)

    @pl.loop(0, 6)
    def _(i):
        start = pl.multiple_of(i * 128, 128)
        r, c = iota((128, 768), 0) + start, iota((128, 768), 1)
        origin = (z_lo + 36 - c // 384 * 8 - c % 96 // 12) % 16
        swap[pl.ds(start, 128)] = (origin * 48 + c % 384 // 96 * 12 + c % 12 == r).astype(BF16)
        tail = r - 512
        part = jnp.where(r < 512, r // 128, tail // 64)
        q = jnp.where(r < 512, r % 128, tail % 64 + 128)
        source = q % 48 // 12 * 192 + q // 48 * 48 + part * 12 + q % 12
        spread[pl.ds(start, 128)] = (source == c).astype(BF16)

    def prepare(p):
        @pl.loop(0, 4)
        def _(part):
            rows = pl.ds(pl.multiple_of(part * 192, 192), 192)
            moved = dot(screened[p, rows], swap[...]).astype(BF16)
            for zh in range(2):
                for other in range(2):
                    half = (other + core + 1) % 2
                    to = pl.multiple_of(half * 384 + part * 96 + zh * 48, 16)
                    at = zh * 96 + other * 48
                    left[p, pl.ds(to, 48)] = moved[at : at + 48]
            right[p, rows] = dot(spread[rows], screened[p]).astype(BF16)

    def plane_copy(g, n):
        mine = dens.at[core, x, pl.ds(pl.multiple_of(g * 384 + y * 96, 16), 96)]
        return remote(
            mine, mine, ps.at[g, n], pr.at[(g * 3 + x) * 4 + y], in_plane(*PLANE[n])
        )

    def spread_plane(g):
        mine = pl.ds(pl.multiple_of(g * 384 + y * 96, 16), 96)
        rows = tile[g * 8 : g * 8 + 8].reshape(128, 128)
        dens[core, x, mine] = dot(squeeze[...], rows).astype(BF16)
        for n in range(len(PLANE)):
            plane_copy(g, n).start()

    @pl.when(x < 3)
    def _():
        for n in (5, 6, 7):
            z_copy(n).wait()
        z_up.start()
        for n in (3, 2, 1, 0):
            z_copy(n).wait()
        z_down.start()
        spread_plane(0)

    prepare(0)

    @pl.when(x < 3)
    def _():
        z_up.wait()
        z_down.wait()
        spread_plane(1)

    prepare(1)
    pl.semaphore_wait(ready, 2)
    for d in (-8, 8):
        pl.semaphore_signal(ready_far, inc=1, device_id=at_z(d), device_id_type=MESH)

    c_copies = []
    for g in range(2):
        for sx in range(3):
            for sy in range(4):
                block = dens.at[core, sx, pl.ds(g * 384 + sy * 96, 96)]

                @pl.when(jnp.logical_or(x != sx, y != sy))
                def _():
                    remote(
                        block, block, ps.at[0, 0], pr.at[(g * 3 + sx) * 4 + sy], sibling
                    ).wait_recv()

            whole = dens.at[core, sx, pl.ds(g * 384, 384)]
            c_copies.append(remote(whole, whole, cs.at[g * 3 + sx], cr.at[g * 3 + sx], sibling))
            c_copies[-1].start()

    def contract(half):
        density = jnp.concatenate([dens[half, t] for t in range(3)], axis=1)

        @pl.loop(0, 4)
        def _(i):
            p, rows = i // 2, pl.ds(pl.multiple_of(i % 2 * 384, 384), 384)
            contracted[p, half, rows] = dot(left[p, rows], density).astype(BF16)

    contract(core)
    for g in range(2):
        for sx in range(3):
            whole = dens.at[1 - core, sx, pl.ds(g * 384, 384)]
            remote(
                whole, whole, cs.at[g * 3 + sx], cr.at[g * 3 + sx], sibling
            ).wait_recv()
    contract(1 - core)

    def exchange(half, chunk):
        total = None
        for p in range(2):
            rows = pl.ds(half * 384, 384)
            a = jnp.concatenate([contracted[p, 0, rows], contracted[p, 1, rows]], axis=1)
            term = dot_nt(a, right[p, pl.ds(chunk * 256, 256)])
            total = term if total is None else total + term
        return total

    k_copies = [
        remote(k_send.at[n], k_land.at[n], ks.at[n], kr.at[n], sibling) for n in range(3)
    ]
    low = iota((48, 128), 1) < 64

    def send_half(n):
        k_send[n] = exchange(0, n).astype(BF16)
        k_copies[n].start()

    def own_half(n):
        own = exchange(1, n)
        k_copies[n].wait_recv()
        total = own + k_land[n].astype(F32)
        for tx in range(4):
            for half in range(2):
                block = total[tx * 96 : tx * 96 + 96, half * 128 : half * 128 + 128]
                if n < 2:
                    p_send[tx * 4 + n * 2 + half, :96] = block.astype(BF16)
                else:
                    first, second = block[:48], block[48:]
                    even = jnp.where(low, first, pltpu.roll(second, 64, 1))
                    odd = jnp.where(low, pltpu.roll(first, 64, 1), second)
                    p_send[tx * 4 + half * 2, 96:] = even.astype(BF16)
                    p_send[tx * 4 + half * 2 + 1, 96:] = odd.astype(BF16)

    parts = [pl.ds(0, 96), pl.ds(96, 48)]

    def send_plane(part, ty):
        for tx in range(4):

            @pl.when(jnp.logical_or(tx != x, ty != y))
            def _():
                slot = (tx - x + 4) % 4 * 4 + (ty - y + 4) % 4
                remote(
                    p_send.at[tx * 4 + ty, parts[part]], p_land.at[slot, parts[part]],
                    qs.at[part, slot], qr.at[part, slot], device(tx, ty, z, core),
                ).start()

    send_half(0)
    send_half(1)
    own_half(0)
    send_plane(0, 0)
    send_plane(0, 1)
    send_half(2)
    own_half(1)
    send_plane(0, 2)
    send_plane(0, 3)
    own_half(2)
    for ty in range(4):
        send_plane(1, ty)

    q_copies = [
        remote(
            p_send.at[0, rows], p_land.at[slot, rows], qs.at[part, slot], qr.at[part, slot], sibling
        )
        for part, rows in enumerate(parts)
        for slot in range(1, 16)
    ]
    sums = []
    for part, rows in enumerate(parts):
        total = p_send[x * 4 + y, rows].astype(F32)
        for slot in range(1, 16):
            q_copies[part * 15 + slot - 1].wait_recv()
            total = total + p_land[slot, rows].astype(F32)
        sums.append(total)

    zeros = jnp.zeros((80, 128), F32)
    by_column[:128] = jnp.transpose(jnp.concatenate([sums[0], zeros[:32]], axis=0))
    turned = jnp.transpose(jnp.concatenate([sums[1], zeros], axis=0))
    lanes = iota((64, 128), 1)
    by_column[128:] = jnp.where(lanes < 48, turned[:64], pltpu.roll(turned[64:], 48, 1))

    n_copies = []
    for n, d in enumerate(Z_NEAR):
        at = pl.multiple_of((z + d + 32) % 4 * 48, 16)
        n_copies.append(
            remote(by_column.at[pl.ds(at, 48)], n_land.at[n], ns.at[n], nr.at[n], at_z(d))
        )
        n_copies[-1].start()
    total = by_column[pl.ds(pl.multiple_of(z % 4 * 48, 16), 48)]
    for n, copy in enumerate(n_copies):
        copy.wait_recv()
        total = total + n_land[n]

    lanes = iota((8, 128), 1)
    for b in range(4):
        first = total[b * 12 : b * 12 + 8]
        second = jnp.concatenate([total[b * 12 + 8 : b * 12 + 12]] * 2, axis=0)
        f_send[b] = jnp.where(lanes < 48, first, pltpu.roll(second, 48, 1))
        f_send[4 + b] = jnp.where(lanes < 48, pltpu.roll(first, 80, 1), second)
    pl.semaphore_wait(ready_far, 2)
    f_copies = []
    for n, d in enumerate(Z_FAR):
        target = wrap(z + d, 32) // 4
        f_copies.append(
            remote(f_send.at[target], f_land.at[n], fs.at[n], fr.at[n], at_z(d))
        )
        f_copies[-1].start()
    total = f_send[z // 4]
    for n, copy in enumerate(f_copies):
        copy.wait_recv()
        total = total + f_land[n]
    out_ref[:8] = total[:, :48]
    out_ref[8:] = pltpu.roll(total, 80, 1)[:4, :48]

    @pl.when(x < 3)
    def _():
        for g in range(2):
            for n in range(len(PLANE)):
                plane_copy(g, n).wait_send()

    for copy in c_copies + k_copies + q_copies + n_copies + f_copies:
        copy.wait_send()


def shards(integrals, block_mask, block_sizes, density):
    dma = lambda *shape: pltpu.SemaphoreType.DMA(shape)
    vmem = lambda *shape: pltpu.VMEM(shape, BF16)
    exchange = pl.pallas_call(
        kernel,
        out_shape=pltpu.VMEM((12, 48), F32),
        in_specs=[pl.BlockSpec(memory_space=pltpu.HBM)] * 4,
        out_specs=pl.BlockSpec(memory_space=pltpu.VMEM),
        scratch_shapes=[
            pltpu.SMEM((6, 2, 6), jnp.int32),
            pltpu.SMEM((6,), jnp.int32),
            vmem(12, 768),
            vmem(2, 768, 768),
            vmem(2, 768, 768),
            vmem(2, 768, 768),
            vmem(2, 768, 768),
            vmem(768, 768),
            vmem(768, 768),
            vmem(96, 128),
            vmem(16, 16, 128),
            vmem(2, 3, 768, 128),
            vmem(2, 2, 768, 384),
            vmem(3, 384, 256),
            vmem(3, 384, 256),
            vmem(16, 144, 128),
            vmem(16, 144, 128),
            pltpu.VMEM((192, 128), F32),
            pltpu.VMEM((3, 48, 128), F32),
            pltpu.VMEM((8, 8, 128), F32),
            pltpu.VMEM((7, 8, 128), F32),
            dma(4),
            pltpu.SemaphoreType.REGULAR,
            pltpu.SemaphoreType.REGULAR,
            dma(10), dma(10),
            dma(2, 15), dma(24),
            dma(6), dma(6),
            dma(3), dma(3),
            dma(2, 16), dma(2, 16),
            dma(3), dma(3),
            dma(7), dma(7),
        ],
        compiler_params=pltpu.CompilerParams(
            collective_id=0, has_side_effects=True, vmem_limit_bytes=60 * 1024 * 1024
        ),
        name="exchange",
    )(jnp.transpose(block_mask, (1, 0, 2)), block_sizes, integrals, density)
    return jnp.transpose(exchange)


def solution(mesh):
    return jax.shard_map(
        shards,
        mesh=mesh,
        in_specs=(
            P(("row", "col"), None, None),
            P(("row", "col"), None, None),
            P(),
            P("col", None),
        ),
        out_specs=P("row", "col"),
        check_vma=False,
    )
```

```python
import jax
import jax.numpy as jnp
from jax import lax
from jax.experimental import pallas as pl
from jax.experimental.pallas import tpu as pltpu
from jax.sharding import PartitionSpec as P

MESH = pl.DeviceIdType.MESH
F32 = jnp.float32
BF16 = jnp.bfloat16

Z_OWN = 4
PLANE = [(dx, dy) for dx in range(4) for dy in range(4) if (dx, dy) != (0, 0)]
Z_NEAR = [-2, -1, 1]
Z_FAR = [-12, -8, -4, 4, 8, 12, 16]
Z_GREET = [-4, 4, -3, 3, -2, 2, -1, 1]


def device(x, y, z, core):
    return ((x * 2 + z // 16) * 2 + core, (z % 16) * 4 + y)


def wrap(value, size):
    return lax.rem(value + size, size)


def iota(shape, dim):
    return lax.broadcasted_iota(jnp.int32, shape, dim)


def dot(a, b):
    return jnp.dot(a, b, preferred_element_type=F32)


def dot_nt(a, b):
    return lax.dot_general(a, b, (((1,), (1,)), ((), ())), preferred_element_type=F32)


def kernel(
    mask_hbm, sizes_hbm, integrals_ref, density_hbm, out_ref,
    mask_ref, sizes_ref, density_ref,
    raw, screened, left, right, swap, spread, squeeze, tile, dens, partial, contracted,
    k_send, k_land, p_send, p_land, by_column, n_land, f_send, f_land,
    load_sem, ready, ready_far, zs, zr, ps, pr, cs, cr, ks, kr, qs, qr, ns, nr, fs, fr,
):
    row, col = lax.axis_index("row"), lax.axis_index("col")
    x, y = row // 4, col % 4
    z, core = (row // 2) % 2 * 16 + col // 4, row % 2
    z_lo = col // 4
    sibling = device(x, y, z, 1 - core)

    def at_z(d):
        return device(x, y, wrap(z + d, 32), core)

    def in_plane(dx, dy):
        return device((x + dx) % 4, (y + dy) % 4, z, core)

    def remote(src, dst, send, recv, target):
        return pltpu.make_async_remote_copy(
            src_ref=src, dst_ref=dst, send_sem=send, recv_sem=recv,
            device_id=target, device_id_type=MESH,
        )

    barrier = pltpu.get_barrier_semaphore()
    greet = [at_z(d) for d in Z_GREET] + [in_plane(*d) for d in PLANE] + [sibling]
    for target in greet:
        pl.semaphore_signal(barrier, inc=1, device_id=target, device_id_type=MESH)

    loads = [
        pltpu.make_async_copy(density_hbm, density_ref, load_sem.at[0]),
        pltpu.make_async_copy(sizes_hbm, sizes_ref, load_sem.at[1]),
        pltpu.make_async_copy(mask_hbm, mask_ref, load_sem.at[2]),
        pltpu.make_async_copy(integrals_ref, raw, load_sem.at[3]),
    ]
    for load in loads:
        load.start()

    r, c = iota((96, 128), 0), iota((96, 128), 1)
    squeeze[...] = ((r // 12) * 16 + r % 12 == c).astype(BF16)

    loads[0].wait()
    column = pl.multiple_of(core * 384 + lax.rem(x, 3) * 128, 128)
    pad = (iota((16, 12), 0) == iota((16, 12), 1)).astype(BF16)
    tile[Z_OWN] = dot(pad, density_ref[:, pl.ds(column, 128)]).astype(BF16)

    pl.semaphore_wait(barrier, len(greet))
    for d in (-4, 4):
        pl.semaphore_signal(ready, inc=1, device_id=at_z(d), device_id_type=MESH)

    def z_copy(n):
        return remote(tile.at[Z_OWN], tile.at[n], zs.at[n], zr.at[n], at_z(n - 4))

    z_up = remote(tile.at[pl.ds(4, 4)], tile.at[pl.ds(8, 4)], zs.at[8], zr.at[8], at_z(4))
    z_down = remote(tile.at[pl.ds(0, 4)], tile.at[pl.ds(12, 4)], zs.at[9], zr.at[9], at_z(-4))

    @pl.when(x < 3)
    def _():
        for n in (0, 1, 7, 2, 6, 3, 5):
            z_copy(n).start()

    for load in loads[1:]:
        load.wait()

    lane = iota((1, 128), 1)
    for i in range(6):
        present_row = (iota((128, 128), 0) < sizes_ref[i]).astype(F32).astype(BF16)
        for p in range(2):
            for k in range(6):
                keep = (lane < sizes_ref[k] * mask_ref[i, p, k]).astype(F32).astype(BF16)
                block = raw[p, pl.ds(i * 128, 128), pl.ds(k * 128, 128)]
                screened[p, pl.ds(i * 128, 128), pl.ds(k * 128, 128)] = block * (present_row * keep)

    @pl.loop(0, 6)
    def _(i):
        start = pl.multiple_of(i * 128, 128)
        r, c = iota((128, 768), 0) + start, iota((128, 768), 1)
        origin = (z_lo + 36 - c // 384 * 8 - c % 96 // 12) % 16
        swap[pl.ds(start, 128)] = (origin * 48 + c % 384 // 96 * 12 + c % 12 == r).astype(BF16)
        tail = r - 512
        part = jnp.where(r < 512, r // 128, tail // 64)
        q = jnp.where(r < 512, r % 128, tail % 64 + 128)
        source = q % 48 // 12 * 192 + q // 48 * 48 + part * 12 + q % 12
        spread[pl.ds(start, 128)] = (source == c).astype(BF16)

    def prepare(p):
        @pl.loop(0, 4)
        def _(part):
            rows = pl.ds(pl.multiple_of(part * 192, 192), 192)
            moved = dot(screened[p, rows], swap[...]).astype(BF16)
            for zh in range(2):
                for other in range(2):
                    half = (other + core + 1) % 2
                    to = pl.multiple_of(half * 384 + part * 96 + zh * 48, 16)
                    at = zh * 96 + other * 48
                    left[p, pl.ds(to, 48)] = moved[at : at + 48]
            right[p, rows] = dot(spread[rows], screened[p]).astype(BF16)

    def plane_copy(g, n):
        mine = dens.at[core, x, pl.ds(pl.multiple_of(g * 384 + y * 96, 16), 96)]
        return remote(
            mine, mine, ps.at[g, n], pr.at[(g * 3 + x) * 4 + y], in_plane(*PLANE[n])
        )

    def spread_plane(g):
        mine = pl.ds(pl.multiple_of(g * 384 + y * 96, 16), 96)
        rows = tile[g * 8 : g * 8 + 8].reshape(128, 128)
        dens[core, x, mine] = dot(squeeze[...], rows).astype(BF16)
        for n in range(len(PLANE)):
            plane_copy(g, n).start()

    @pl.when(x < 3)
    def _():
        for n in (5, 6, 7):
            z_copy(n).wait()
        z_up.start()
        for n in (3, 2, 1, 0):
            z_copy(n).wait()
        z_down.start()
        spread_plane(0)

    prepare(0)

    @pl.when(x < 3)
    def _():
        z_up.wait()
        z_down.wait()
        spread_plane(1)

    prepare(1)
    pl.semaphore_wait(ready, 2)
    for d in (-8, 8):
        pl.semaphore_signal(ready_far, inc=1, device_id=at_z(d), device_id_type=MESH)

    def pass_on(g, sx, to):
        whole = dens.at[to, sx, pl.ds(g * 384, 384)]
        return remote(whole, whole, cs.at[g * 3 + sx], cr.at[g * 3 + sx], sibling)

    def pass_group(g):
        for sx in range(3):
            for sy in range(4):
                block = dens.at[core, sx, pl.ds(g * 384 + sy * 96, 96)]

                @pl.when(jnp.logical_or(x != sx, y != sy))
                def _():
                    remote(
                        block, block, ps.at[0, 0], pr.at[(g * 3 + sx) * 4 + sy], sibling
                    ).wait_recv()

            pass_on(g, sx, core).start()

    def await_group(g):
        for sx in range(3):
            pass_on(g, sx, 1 - core).wait_recv()

    def contract(half, g, rows_of):
        @pl.loop(0, 2)
        def _(p):
            rows, depth = pl.ds(rows_of * 384, 384), pl.ds(g * 384, 384)
            density = jnp.concatenate([dens[half, t, depth] for t in range(3)], axis=1)
            term = dot(left[p, rows, depth], density)
            if g == 0:
                partial[p, half, rows] = term
            else:
                contracted[p, half, rows] = (partial[p, half, rows] + term).astype(BF16)

    pass_group(0)
    contract(core, 0, 0)
    contract(core, 0, 1)
    await_group(0)
    contract(1 - core, 0, 0)
    contract(1 - core, 0, 1)
    pass_group(1)
    contract(core, 1, 0)
    contract(core, 1, 1)
    await_group(1)
    contract(1 - core, 1, 0)

    def exchange(half, chunk):
        total = None
        for p in range(2):
            rows = pl.ds(half * 384, 384)
            a = jnp.concatenate([contracted[p, 0, rows], contracted[p, 1, rows]], axis=1)
            term = dot_nt(a, right[p, pl.ds(chunk * 256, 256)])
            total = term if total is None else total + term
        return total

    k_copies = [
        remote(k_send.at[n], k_land.at[n], ks.at[n], kr.at[n], sibling) for n in range(3)
    ]
    low = iota((48, 128), 1) < 64

    def send_half(n):
        k_send[n] = exchange(0, n).astype(BF16)
        k_copies[n].start()

    def own_half(n):
        own = exchange(1, n)
        k_copies[n].wait_recv()
        total = own + k_land[n].astype(F32)
        for tx in range(4):
            for half in range(2):
                block = total[tx * 96 : tx * 96 + 96, half * 128 : half * 128 + 128]
                if n < 2:
                    p_send[tx * 4 + n * 2 + half, :96] = block.astype(BF16)
                else:
                    first, second = block[:48], block[48:]
                    even = jnp.where(low, first, pltpu.roll(second, 64, 1))
                    odd = jnp.where(low, pltpu.roll(first, 64, 1), second)
                    p_send[tx * 4 + half * 2, 96:] = even.astype(BF16)
                    p_send[tx * 4 + half * 2 + 1, 96:] = odd.astype(BF16)

    parts = [pl.ds(0, 96), pl.ds(96, 48)]

    def send_plane(part, ty):
        for tx in range(4):

            @pl.when(jnp.logical_or(tx != x, ty != y))
            def _():
                slot = (tx - x + 4) % 4 * 4 + (ty - y + 4) % 4
                remote(
                    p_send.at[tx * 4 + ty, parts[part]], p_land.at[slot, parts[part]],
                    qs.at[part, slot], qr.at[part, slot], device(tx, ty, z, core),
                ).start()

    send_half(0)
    contract(1 - core, 1, 1)
    own_half(0)
    send_plane(0, 0)
    send_plane(0, 1)
    send_half(1)
    send_half(2)
    own_half(1)
    send_plane(0, 2)
    send_plane(0, 3)
    own_half(2)
    for ty in range(4):
        send_plane(1, ty)

    q_copies = [
        remote(
            p_send.at[0, rows], p_land.at[slot, rows], qs.at[part, slot], qr.at[part, slot], sibling
        )
        for part, rows in enumerate(parts)
        for slot in range(1, 16)
    ]
    sums = []
    for part, rows in enumerate(parts):
        total = p_send[x * 4 + y, rows].astype(F32)
        for slot in range(1, 16):
            q_copies[part * 15 + slot - 1].wait_recv()
            total = total + p_land[slot, rows].astype(F32)
        sums.append(total)

    zeros = jnp.zeros((80, 128), F32)
    by_column[:128] = jnp.transpose(jnp.concatenate([sums[0], zeros[:32]], axis=0))
    turned = jnp.transpose(jnp.concatenate([sums[1], zeros], axis=0))
    lanes = iota((64, 128), 1)
    by_column[128:] = jnp.where(lanes < 48, turned[:64], pltpu.roll(turned[64:], 48, 1))

    n_copies = []
    for n, d in enumerate(Z_NEAR):
        at = pl.multiple_of((z + d + 32) % 4 * 48, 16)
        n_copies.append(
            remote(by_column.at[pl.ds(at, 48)], n_land.at[n], ns.at[n], nr.at[n], at_z(d))
        )
        n_copies[-1].start()
    total = by_column[pl.ds(pl.multiple_of(z % 4 * 48, 16), 48)]
    for n, copy in enumerate(n_copies):
        copy.wait_recv()
        total = total + n_land[n]

    lanes = iota((8, 128), 1)
    for b in range(4):
        first = total[b * 12 : b * 12 + 8]
        second = jnp.concatenate([total[b * 12 + 8 : b * 12 + 12]] * 2, axis=0)
        f_send[b] = jnp.where(lanes < 48, first, pltpu.roll(second, 48, 1))
        f_send[4 + b] = jnp.where(lanes < 48, pltpu.roll(first, 80, 1), second)
    pl.semaphore_wait(ready_far, 2)
    f_copies = []
    for n, d in enumerate(Z_FAR):
        target = wrap(z + d, 32) // 4
        f_copies.append(
            remote(f_send.at[target], f_land.at[n], fs.at[n], fr.at[n], at_z(d))
        )
        f_copies[-1].start()
    total = f_send[z // 4]
    for n, copy in enumerate(f_copies):
        copy.wait_recv()
        total = total + f_land[n]
    out_ref[:8] = total[:, :48]
    out_ref[8:] = pltpu.roll(total, 80, 1)[:4, :48]

    @pl.when(x < 3)
    def _():
        for g in range(2):
            for n in range(len(PLANE)):
                plane_copy(g, n).wait_send()

    for n in range(6):
        pass_on(n // 3, n % 3, core).wait_send()
    for copy in k_copies + q_copies + n_copies + f_copies:
        copy.wait_send()


def shards(integrals, block_mask, block_sizes, density):
    dma = lambda *shape: pltpu.SemaphoreType.DMA(shape)
    vmem = lambda *shape: pltpu.VMEM(shape, BF16)
    exchange = pl.pallas_call(
        kernel,
        out_shape=pltpu.VMEM((12, 48), F32),
        in_specs=[pl.BlockSpec(memory_space=pltpu.HBM)] * 4,
        out_specs=pl.BlockSpec(memory_space=pltpu.VMEM),
        scratch_shapes=[
            pltpu.SMEM((6, 2, 6), jnp.int32),
            pltpu.SMEM((6,), jnp.int32),
            vmem(12, 768),
            vmem(2, 768, 768),
            vmem(2, 768, 768),
            vmem(2, 768, 768),
            vmem(2, 768, 768),
            vmem(768, 768),
            vmem(768, 768),
            vmem(96, 128),
            vmem(16, 16, 128),
            vmem(2, 3, 768, 128),
            pltpu.VMEM((2, 2, 768, 384), F32),
            vmem(2, 2, 768, 384),
            vmem(3, 384, 256),
            vmem(3, 384, 256),
            vmem(16, 144, 128),
            vmem(16, 144, 128),
            pltpu.VMEM((192, 128), F32),
            pltpu.VMEM((3, 48, 128), F32),
            pltpu.VMEM((8, 8, 128), F32),
            pltpu.VMEM((7, 8, 128), F32),
            dma(4),
            pltpu.SemaphoreType.REGULAR,
            pltpu.SemaphoreType.REGULAR,
            dma(10), dma(10),
            dma(2, 15), dma(24),
            dma(6), dma(6),
            dma(3), dma(3),
            dma(2, 16), dma(2, 16),
            dma(3), dma(3),
            dma(7), dma(7),
        ],
        compiler_params=pltpu.CompilerParams(
            collective_id=0, has_side_effects=True, vmem_limit_bytes=60 * 1024 * 1024
        ),
        name="exchange",
    )(jnp.transpose(block_mask, (1, 0, 2)), block_sizes, integrals, density)
    return jnp.transpose(exchange)


def solution(mesh):
    return jax.shard_map(
        shards,
        mesh=mesh,
        in_specs=(
            P(("row", "col"), None, None),
            P(("row", "col"), None, None),
            P(),
            P("col", None),
        ),
        out_specs=P("row", "col"),
        check_vma=False,
    )
```

```python
import jax
import jax.numpy as jnp
from jax import lax
from jax.experimental import pallas as pl
from jax.experimental.pallas import tpu as pltpu
from jax.sharding import PartitionSpec as P

MESH = pl.DeviceIdType.MESH
F32 = jnp.float32
BF16 = jnp.bfloat16

Z_OWN = 4
FARTHEST = (2, 1, 3, 0)
PLANE = [(dx, dy) for dx in FARTHEST for dy in FARTHEST if (dx, dy) != (0, 0)]
Z_NEAR = [-2, -1, 1]
Z_FAR = [16, 12, -12, 8, -8, 4, -4]
Z_GREET = [-4, 4, -3, 3, -2, 2, -1, 1]


def device(x, y, z, core):
    return ((x * 2 + z // 16) * 2 + core, (z % 16) * 4 + y)


def wrap(value, size):
    return lax.rem(value + size, size)


def iota(shape, dim):
    return lax.broadcasted_iota(jnp.int32, shape, dim)


def dot(a, b):
    return jnp.dot(a, b, preferred_element_type=F32)


def dot_nt(a, b):
    return lax.dot_general(a, b, (((1,), (1,)), ((), ())), preferred_element_type=F32)


def kernel(
    mask_hbm, sizes_hbm, integrals_ref, density_hbm, out_ref,
    mask_ref, sizes_ref, density_ref,
    raw, screened, left, right, swap, spread, squeeze, tile, dens, partial, contracted,
    k_send, k_land, p_send, p_land, by_column, n_land, f_send, f_land,
    load_sem, ready, ready_far, zs, zr, ps, pr, cs, cr, ks, kr, qs, qr, ns, nr, fs, fr,
):
    row, col = lax.axis_index("row"), lax.axis_index("col")
    x, y = row // 4, col % 4
    z, core = (row // 2) % 2 * 16 + col // 4, row % 2
    z_lo = col // 4
    sibling = device(x, y, z, 1 - core)

    def at_z(d):
        return device(x, y, wrap(z + d, 32), core)

    def in_plane(dx, dy):
        return device((x + dx) % 4, (y + dy) % 4, z, core)

    def remote(src, dst, send, recv, target):
        return pltpu.make_async_remote_copy(
            src_ref=src, dst_ref=dst, send_sem=send, recv_sem=recv,
            device_id=target, device_id_type=MESH,
        )

    barrier = pltpu.get_barrier_semaphore()
    greet = [at_z(d) for d in Z_GREET] + [in_plane(*d) for d in PLANE] + [sibling]
    for target in greet:
        pl.semaphore_signal(barrier, inc=1, device_id=target, device_id_type=MESH)

    loads = [
        pltpu.make_async_copy(density_hbm, density_ref, load_sem.at[0]),
        pltpu.make_async_copy(sizes_hbm, sizes_ref, load_sem.at[1]),
        pltpu.make_async_copy(mask_hbm, mask_ref, load_sem.at[2]),
        pltpu.make_async_copy(integrals_ref, raw, load_sem.at[3]),
    ]
    for load in loads:
        load.start()

    r, c = iota((96, 128), 0), iota((96, 128), 1)
    squeeze[...] = ((r // 12) * 16 + r % 12 == c).astype(BF16)

    loads[0].wait()
    column = pl.multiple_of(core * 384 + lax.rem(x, 3) * 128, 128)
    pad = (iota((16, 12), 0) == iota((16, 12), 1)).astype(BF16)
    tile[Z_OWN] = dot(pad, density_ref[:, pl.ds(column, 128)]).astype(BF16)

    pl.semaphore_wait(barrier, len(greet))
    for d in (-4, 4):
        pl.semaphore_signal(ready, inc=1, device_id=at_z(d), device_id_type=MESH)

    def z_copy(n):
        return remote(tile.at[Z_OWN], tile.at[n], zs.at[n], zr.at[n], at_z(n - 4))

    z_up = remote(tile.at[pl.ds(4, 4)], tile.at[pl.ds(8, 4)], zs.at[8], zr.at[8], at_z(4))
    z_down = remote(tile.at[pl.ds(0, 4)], tile.at[pl.ds(12, 4)], zs.at[9], zr.at[9], at_z(-4))

    @pl.when(x < 3)
    def _():
        for n in (0, 1, 7, 2, 6, 3, 5):
            z_copy(n).start()

    for load in loads[1:]:
        load.wait()

    lane = iota((1, 128), 1)
    for i in range(6):
        present_row = (iota((128, 128), 0) < sizes_ref[i]).astype(F32).astype(BF16)
        for p in range(2):
            for k in range(6):
                keep = (lane < sizes_ref[k] * mask_ref[i, p, k]).astype(F32).astype(BF16)
                block = raw[p, pl.ds(i * 128, 128), pl.ds(k * 128, 128)]
                screened[p, pl.ds(i * 128, 128), pl.ds(k * 128, 128)] = block * (present_row * keep)

    @pl.loop(0, 6)
    def _(i):
        start = pl.multiple_of(i * 128, 128)
        r, c = iota((128, 768), 0) + start, iota((128, 768), 1)
        origin = (z_lo + 36 - c // 384 * 8 - c % 96 // 12) % 16
        swap[pl.ds(start, 128)] = (origin * 48 + c % 384 // 96 * 12 + c % 12 == r).astype(BF16)
        tail = r - 512
        part = (y + 6 - jnp.where(r < 512, r // 128, tail // 64)) % 4
        q = jnp.where(r < 512, r % 128, tail % 64 + 128)
        source = q % 48 // 12 * 192 + q // 48 * 48 + part * 12 + q % 12
        spread[pl.ds(start, 128)] = (source == c).astype(BF16)

    def prepare(p):
        @pl.loop(0, 4)
        def _(part):
            rows = pl.ds(pl.multiple_of(part * 192, 192), 192)
            moved = dot(screened[p, rows], swap[...]).astype(BF16)
            for zh in range(2):
                for other in range(2):
                    half = (other + core + 1) % 2
                    to = pl.multiple_of(half * 384 + part * 96 + zh * 48, 16)
                    at = zh * 96 + other * 48
                    left[p, pl.ds(to, 48)] = moved[at : at + 48]
            right[p, rows] = dot(spread[rows], screened[p]).astype(BF16)

    def plane_copy(g, n):
        mine = dens.at[core, x, pl.ds(pl.multiple_of(g * 384 + y * 96, 16), 96)]
        return remote(
            mine, mine, ps.at[g, n], pr.at[(g * 3 + x) * 4 + y], in_plane(*PLANE[n])
        )

    def spread_plane(g):
        mine = pl.ds(pl.multiple_of(g * 384 + y * 96, 16), 96)
        rows = tile[g * 8 : g * 8 + 8].reshape(128, 128)
        dens[core, x, mine] = dot(squeeze[...], rows).astype(BF16)
        for n in range(len(PLANE)):
            plane_copy(g, n).start()

    @pl.when(x < 3)
    def _():
        for n in (5, 6, 7):
            z_copy(n).wait()
        z_up.start()
        for n in (3, 2, 1, 0):
            z_copy(n).wait()
        z_down.start()
        spread_plane(0)

    prepare(0)

    @pl.when(x < 3)
    def _():
        z_up.wait()
        z_down.wait()
        spread_plane(1)

    prepare(1)
    pl.semaphore_wait(ready, 2)
    for d in (-8, 8):
        pl.semaphore_signal(ready_far, inc=1, device_id=at_z(d), device_id_type=MESH)

    def pass_on(g, sx, to):
        whole = dens.at[to, sx, pl.ds(g * 384, 384)]
        return remote(whole, whole, cs.at[g * 3 + sx], cr.at[g * 3 + sx], sibling)

    def pass_group(g):
        for sx in range(3):
            for sy in range(4):
                block = dens.at[core, sx, pl.ds(g * 384 + sy * 96, 96)]

                @pl.when(jnp.logical_or(x != sx, y != sy))
                def _():
                    remote(
                        block, block, ps.at[0, 0], pr.at[(g * 3 + sx) * 4 + sy], sibling
                    ).wait_recv()

            pass_on(g, sx, core).start()

    def await_group(g):
        for sx in range(3):
            pass_on(g, sx, 1 - core).wait_recv()

    def contract(half, g, rows_of):
        @pl.loop(0, 2)
        def _(p):
            rows, depth = pl.ds(rows_of * 384, 384), pl.ds(g * 384, 384)
            density = jnp.concatenate([dens[half, t, depth] for t in range(3)], axis=1)
            term = dot(left[p, rows, depth], density)
            if g == 0:
                partial[p, half, rows] = term
            else:
                contracted[p, half, rows] = (partial[p, half, rows] + term).astype(BF16)

    pass_group(0)
    contract(core, 0, 0)
    contract(core, 0, 1)
    await_group(0)
    contract(1 - core, 0, 0)
    contract(1 - core, 0, 1)
    pass_group(1)
    contract(core, 1, 0)
    contract(core, 1, 1)
    await_group(1)
    contract(1 - core, 1, 0)

    def exchange(half, chunk):
        total = None
        for p in range(2):
            rows = pl.ds(half * 384, 384)
            a = jnp.concatenate([contracted[p, 0, rows], contracted[p, 1, rows]], axis=1)
            term = dot_nt(a, right[p, pl.ds(chunk * 256, 256)])
            total = term if total is None else total + term
        return total

    k_copies = [
        remote(k_send.at[n], k_land.at[n], ks.at[n], kr.at[n], sibling) for n in range(3)
    ]
    low = iota((48, 128), 1) < 64

    def send_half(n):
        k_send[n] = exchange(0, n).astype(BF16)
        k_copies[n].start()

    def own_half(n):
        own = exchange(1, n)
        k_copies[n].wait_recv()
        total = own + k_land[n].astype(F32)
        for tx in range(4):
            for half in range(2):
                block = total[tx * 96 : tx * 96 + 96, half * 128 : half * 128 + 128]
                if n < 2:
                    p_send[tx * 4 + n * 2 + half, :96] = block.astype(BF16)
                else:
                    first, second = block[:48], block[48:]
                    even = jnp.where(low, first, pltpu.roll(second, 64, 1))
                    odd = jnp.where(low, pltpu.roll(first, 64, 1), second)
                    p_send[tx * 4 + half * 2, 96:] = even.astype(BF16)
                    p_send[tx * 4 + half * 2 + 1, 96:] = odd.astype(BF16)

    parts = [pl.ds(0, 96), pl.ds(96, 48)]

    def send_plane(part, k):
        dy = (6 - k) % 4
        for dx in FARTHEST:
            if (dx, dy) != (0, 0):
                slot = dx * 4 + dy
                remote(
                    p_send.at[(x + dx) % 4 * 4 + k, parts[part]], p_land.at[slot, parts[part]],
                    qs.at[part, slot], qr.at[part, slot], in_plane(dx, dy),
                ).start()

    send_half(0)
    contract(1 - core, 1, 1)
    own_half(0)
    send_plane(0, 0)
    send_plane(0, 1)
    send_half(1)
    send_half(2)
    own_half(1)
    send_plane(0, 2)
    send_plane(0, 3)
    own_half(2)
    for k in range(4):
        send_plane(1, k)

    q_copies = [
        remote(
            p_send.at[0, rows], p_land.at[slot, rows], qs.at[part, slot], qr.at[part, slot], sibling
        )
        for part, rows in enumerate(parts)
        for slot in range(1, 16)
    ]
    sums = []
    for part, rows in enumerate(parts):
        total = p_send[x * 4 + 2, rows].astype(F32)
        for slot in range(1, 16):
            q_copies[part * 15 + slot - 1].wait_recv()
            total = total + p_land[slot, rows].astype(F32)
        sums.append(total)

    zeros = jnp.zeros((80, 128), F32)
    by_column[:128] = jnp.transpose(jnp.concatenate([sums[0], zeros[:32]], axis=0))
    turned = jnp.transpose(jnp.concatenate([sums[1], zeros], axis=0))
    lanes = iota((64, 128), 1)
    by_column[128:] = jnp.where(lanes < 48, turned[:64], pltpu.roll(turned[64:], 48, 1))

    n_copies = []
    for n, d in enumerate(Z_NEAR):
        at = pl.multiple_of((z + d + 32) % 4 * 48, 16)
        n_copies.append(
            remote(by_column.at[pl.ds(at, 48)], n_land.at[n], ns.at[n], nr.at[n], at_z(d))
        )
        n_copies[-1].start()
    total = by_column[pl.ds(pl.multiple_of(z % 4 * 48, 16), 48)]
    for n, copy in enumerate(n_copies):
        copy.wait_recv()
        total = total + n_land[n]

    lanes = iota((8, 128), 1)
    for b in range(4):
        first = total[b * 12 : b * 12 + 8]
        second = jnp.concatenate([total[b * 12 + 8 : b * 12 + 12]] * 2, axis=0)
        f_send[b] = jnp.where(lanes < 48, first, pltpu.roll(second, 48, 1))
        f_send[4 + b] = jnp.where(lanes < 48, pltpu.roll(first, 80, 1), second)
    pl.semaphore_wait(ready_far, 2)
    f_copies = []
    for n, d in enumerate(Z_FAR):
        target = wrap(z + d, 32) // 4
        f_copies.append(
            remote(f_send.at[target], f_land.at[n], fs.at[n], fr.at[n], at_z(d))
        )
        f_copies[-1].start()
    total = f_send[z // 4]
    for n, copy in enumerate(f_copies):
        copy.wait_recv()
        total = total + f_land[n]
    out_ref[:8] = total[:, :48]
    out_ref[8:] = pltpu.roll(total, 80, 1)[:4, :48]

    @pl.when(x < 3)
    def _():
        for g in range(2):
            for n in range(len(PLANE)):
                plane_copy(g, n).wait_send()

    for n in range(6):
        pass_on(n // 3, n % 3, core).wait_send()
    for copy in k_copies + q_copies + n_copies + f_copies:
        copy.wait_send()


def shards(integrals, block_mask, block_sizes, density):
    dma = lambda *shape: pltpu.SemaphoreType.DMA(shape)
    vmem = lambda *shape: pltpu.VMEM(shape, BF16)
    exchange = pl.pallas_call(
        kernel,
        out_shape=pltpu.VMEM((12, 48), F32),
        in_specs=[pl.BlockSpec(memory_space=pltpu.HBM)] * 4,
        out_specs=pl.BlockSpec(memory_space=pltpu.VMEM),
        scratch_shapes=[
            pltpu.SMEM((6, 2, 6), jnp.int32),
            pltpu.SMEM((6,), jnp.int32),
            vmem(12, 768),
            vmem(2, 768, 768),
            vmem(2, 768, 768),
            vmem(2, 768, 768),
            vmem(2, 768, 768),
            vmem(768, 768),
            vmem(768, 768),
            vmem(96, 128),
            vmem(16, 16, 128),
            vmem(2, 3, 768, 128),
            pltpu.VMEM((2, 2, 768, 384), F32),
            vmem(2, 2, 768, 384),
            vmem(3, 384, 256),
            vmem(3, 384, 256),
            vmem(16, 144, 128),
            vmem(16, 144, 128),
            pltpu.VMEM((192, 128), F32),
            pltpu.VMEM((3, 48, 128), F32),
            pltpu.VMEM((8, 8, 128), F32),
            pltpu.VMEM((7, 8, 128), F32),
            dma(4),
            pltpu.SemaphoreType.REGULAR,
            pltpu.SemaphoreType.REGULAR,
            dma(10), dma(10),
            dma(2, 15), dma(24),
            dma(6), dma(6),
            dma(3), dma(3),
            dma(2, 16), dma(2, 16),
            dma(3), dma(3),
            dma(7), dma(7),
        ],
        compiler_params=pltpu.CompilerParams(
            collective_id=0, has_side_effects=True, vmem_limit_bytes=60 * 1024 * 1024
        ),
        name="exchange",
    )(jnp.transpose(block_mask, (1, 0, 2)), block_sizes, integrals, density)
    return jnp.transpose(exchange)


def solution(mesh):
    return jax.shard_map(
        shards,
        mesh=mesh,
        in_specs=(
            P(("row", "col"), None, None),
            P(("row", "col"), None, None),
            P(),
            P("col", None),
        ),
        out_specs=P("row", "col"),
        check_vma=False,
    )
```
